128 devices in a mesh: seq: 8 (over z, y_hi), ctx: 16 (over x, y_lo, core).
Axes of the slice: x: 4, y: 4 (y_hi: 2, y_lo: 2; y = y_hi * 2 + y_lo), z: 4, core: 2. Of those that a mesh axis runs over, the one named last changes fastest.
Arguments:
- layer_input: bfloat16 [8, 2048, 2048], P('seq', 'ctx'), may hold values from -6 to 6
- out_cotangent: bfloat16 [8, 2048, 2048], P('seq', 'ctx'), may hold values from -6 to 6
- positions: int32 [8, 2048], P('seq'), may hold values from 0 to 4094, as said below
- qkv_weight: float32 [2048, 2560], P(('seq', 'ctx')), may hold values from -0.15625 to 0.15625
- qkv_first: float32 [2048, 2560], P(('seq', 'ctx')), may hold values from -160 to 160
- qkv_second: float32 [2048, 2560], P(('seq', 'ctx')), may hold values from 3473.408 to 13762.56
- proj_weight: float32 [2048, 2048], P(('seq', 'ctx')), may hold values from -1 to 1
- proj_first: float32 [2048, 2048], P(('seq', 'ctx')), may hold values from -16 to 16
- proj_second: float32 [2048, 2048], P(('seq', 'ctx')), may hold values from 26.712 to 105.84
- gate_up_weight: float32 [2048, 11264], P(('seq', 'ctx')), may hold values from -0.125 to 0.125
- gate_up_first: float32 [2048, 11264], P(('seq', 'ctx')), may hold values from -80 to 80
- gate_up_second: float32 [2048, 11264], P(('seq', 'ctx')), may hold values from 868.352 to 3440.64
- down_weight: float32 [5632, 2048], P(('seq', 'ctx')), may hold values from -0.125 to 0.125
- down_first: float32 [5632, 2048], P(('seq', 'ctx')), may hold values from -48 to 48
- down_second: float32 [5632, 2048], P(('seq', 'ctx')), may hold values from 303.9232 to 1204.224
- norm_gains: float32 [2048, 2], P(('seq', 'ctx')), may hold values from 0.5 to 1.5
- gains_first: float32 [2048, 2], P(('seq', 'ctx')), may hold values from -256 to 256
- gains_second: float32 [2048, 2], P(('seq', 'ctx')), may hold values from 7815.168 to 30965.76
Outputs:
- block_output: bfloat16 [8, 2048, 2048], P('seq', 'ctx')
- input_grad: float32 [8, 2048, 2048], P('seq', 'ctx')
- qkv_first_new: float32 [2048, 2560], P(('seq', 'ctx'))
- qkv_second_new: float32 [2048, 2560], P(('seq', 'ctx'))
- qkv_weight_new: float32 [2048, 2560], P(('seq', 'ctx'))
- proj_first_new: float32 [2048, 2048], P(('seq', 'ctx'))
- proj_second_new: float32 [2048, 2048], P(('seq', 'ctx'))
- proj_weight_new: float32 [2048, 2048], P(('seq', 'ctx'))
- gate_up_first_new: float32 [2048, 11264], P(('seq', 'ctx'))
- gate_up_second_new: float32 [2048, 11264], P(('seq', 'ctx'))
- gate_up_weight_new: float32 [2048, 11264], P(('seq', 'ctx'))
- down_first_new: float32 [5632, 2048], P(('seq', 'ctx'))
- down_second_new: float32 [5632, 2048], P(('seq', 'ctx'))
- down_weight_new: float32 [5632, 2048], P(('seq', 'ctx'))
- gains_first_new: float32 [2048, 2], P(('seq', 'ctx'))
- gains_second_new: float32 [2048, 2], P(('seq', 'ctx'))
- gains_new: float32 [2048, 2], P(('seq', 'ctx'))
The draws below stay inside these ranges and needn't reach their ends.
Inputs may be any that keep to these rules, and one draw needn't show every extreme that they name: Along each sequence's own order the positions start at 0 and rise strictly from token to token, by 1 or 2 except at the last token, which sits at 4094. The array holds each sequence in 32 blocks of 64 tokens; the two blocks stored at slots 2c and 2c+1 are blocks b and 31-b of the sequence's order for some b, in either order.
All inputs are finite; a program needn't handle non-finite values.
Results may differ from the reference program's by a relative error of at most 0.022.
Values may be sent and summed in bfloat16 or wider, within the bound.
No kernel may reach another device: no remote copies, remote signals or barrier semaphores. Data moves between devices by JAX's collectives and lax.ppermute only.
A program may use at most 448 MiB of HBM per device.

```python
import math
import jax
import jax.numpy as jnp
from jax import lax

D = 2048
FF = 5632
HEADS = 32
KV_HEADS = 4
HEAD_DIM = 64
STEP = 10
SEQS = 8
LENGTH = 2048
TOKENS = 16384
BLOCK = 64
BLOCKS = 32
QKV_COLS = 2560


def draw_positions(key, part):
    key = jax.random.fold_in(key, 11)
    key_steps, key_pairs, key_flips = jax.random.split(key, 3)
    steps_int = jax.random.randint(key_steps, (SEQS, LENGTH), 1, 3)
    ordered = jnp.cumsum(steps_int, axis=1) - steps_int[:, :1]
    column_ids = jnp.arange(LENGTH, dtype=jnp.int32)[None, :]
    ordered = jnp.where(column_ids == LENGTH - 1, 2 * LENGTH - 2, ordered)
    pair_keys = jax.random.split(key_pairs, SEQS)
    pairing = jax.vmap(lambda pair_key: jax.random.permutation(pair_key, BLOCKS // 2))(pair_keys)
    flipped = jax.random.randint(key_flips, (SEQS, BLOCKS // 2), 0, 2)
    lower_blk = pairing
    upper_blk = BLOCKS - 1 - pairing
    first_blk = jnp.where(flipped == 1, upper_blk, lower_blk)
    second_blk = jnp.where(flipped == 1, lower_blk, upper_blk)
    slot_order = jnp.stack([first_blk, second_blk], axis=2).reshape(SEQS, BLOCKS).astype(jnp.int32)
    blocked = ordered.reshape(SEQS, BLOCKS, BLOCK)
    dealt = jnp.take_along_axis(blocked, slot_order[:, :, None], axis=1)
    return dealt.reshape(SEQS, LENGTH).astype(jnp.int32)


def strengthened(array, rng, source, target, shards_of, factor):
    def block_of(position):
        return (jnp.arange(array.shape[position]) // (array.shape[position] // shards_of)).reshape((-1,) + (1,) * (array.ndim - 1 - position))

    one_side = jax.random.permutation(rng, shards_of)[block_of(target)]
    other_side = (block_of(target) + shards_of // 2) % shards_of
    return jnp.where((block_of(source) == one_side) | (block_of(source) == other_side), factor * array, array)


def block_levels(stream_key, dims, cuts, least, top_value):
    loudness, own = 1.0, jax.random.fold_in(stream_key, 6)
    for dim, shards_of in cuts:
        draws = jnp.exp(jax.random.uniform(jax.random.fold_in(own, dim), (shards_of,), jnp.float32, least / len(cuts), top_value / len(cuts)))
        loudness = loudness * jnp.repeat(draws, dims[dim] // shards_of).reshape([-1 if axis == dim else 1 for axis in range(len(dims))])
    return loudness


def bell_draw(key, dims, spread, limit, cuts=(), kind=jnp.bfloat16):
    level = block_levels(key, dims, cuts, -0.22, 0.18) if cuts else 1.0
    drawn = jax.random.normal(key, dims, jnp.float32) * spread * level
    return jnp.minimum(jnp.maximum(drawn, -limit), limit).astype(kind)


def heavy_noise(own_key, dims, width, most, pieces, heavy, held_as=jnp.bfloat16):
    entries = width * jax.random.normal(own_key, dims, jnp.float32)
    if pieces:
        entries = entries * block_levels(own_key, dims, pieces, -0.22, 0.18)
    return jnp.clip(strengthened(entries, jax.random.fold_in(own_key, 3), *heavy), -most, most).astype(held_as)


def setup_inputs(seed: int = 0) -> dict:
    streams_of = jax.random.split(jax.random.key(seed), 19)
    return {
        "layer_input": heavy_noise(streams_of[0], (SEQS, LENGTH, D), 1.0, 6.0, ((0, 8), (1, 16)), (1, 2, 16, 2.0)),
        "out_cotangent": heavy_noise(streams_of[1], (SEQS, LENGTH, D), 1.0, 6.0, ((0, 8), (1, 16)), (1, 2, 16, 2.0)),
        "positions": draw_positions(jax.random.fold_in(streams_of[18], 71), 0),
        "qkv_weight": bell_draw(streams_of[3], (D, QKV_COLS), (D * 2 // 3) ** -0.5, 0.15625, ((0, 128),), jnp.float32),
        "qkv_first": bell_draw(streams_of[4], (D, QKV_COLS), (0.111 * (4 * TOKENS) ** 0.5), 160.0, ((0, 128),), jnp.float32),
        "qkv_second": jnp.clip(jnp.exp(math.log(13762.56) - 1.3768156 * jax.random.uniform(streams_of[5], (D, QKV_COLS), jnp.float32) ** block_levels(streams_of[5], (D, QKV_COLS), ((0, 128),), -0.2, 0.2)), 3473.408, 13762.56),
        "proj_weight": bell_draw(streams_of[6], (D, D), (D * 28 // LENGTH) ** -0.5, 1.0, ((0, 128),), jnp.float32),
        "proj_first": bell_draw(streams_of[7], (D, D), (0.111 * (63 * SEQS) ** 0.5), 16.0, ((0, 128),), jnp.float32),
        "proj_second": jnp.clip(jnp.exp(math.log(105.84) - 1.3768156 * jax.random.uniform(streams_of[8], (D, D), jnp.float32) ** block_levels(streams_of[8], (D, D), ((0, 128),), -0.2, 0.2)), 26.712, 105.84),
        "gate_up_weight": bell_draw(streams_of[9], (D, 2 * FF), D ** -0.5, 0.125, ((0, 128),), jnp.float32),
        "gate_up_first": bell_draw(streams_of[10], (D, 2 * FF), (0.111 * TOKENS ** 0.5), 80.0, ((0, 128),), jnp.float32),
        "gate_up_second": jnp.clip(jnp.exp(math.log(3440.64) - 1.3768156 * jax.random.uniform(streams_of[11], (D, 2 * FF), jnp.float32) ** block_levels(streams_of[11], (D, 2 * FF), ((0, 128),), -0.2, 0.2)), 868.352, 3440.64),
        "down_weight": bell_draw(streams_of[12], (FF, D), (FF // 3) ** -0.5, 0.125, ((0, 128),), jnp.float32),
        "down_first": bell_draw(streams_of[13], (FF, D), (0.111 * (0.35 * TOKENS) ** 0.5), 48.0, ((0, 128),), jnp.float32),
        "down_second": jnp.clip(jnp.exp(math.log(1204.224) - 1.3768157 * jax.random.uniform(streams_of[14], (FF, D), jnp.float32) ** block_levels(streams_of[14], (FF, D), ((0, 128),), -0.2, 0.2)), 303.9232, 1204.224),
        "norm_gains": jnp.clip(1.0 + 0.1 * jax.random.normal(streams_of[15], (D, 2), jnp.float32), 0.5, 1.5),
        "gains_first": bell_draw(streams_of[16], (D, 2), (0.111 * (9 * TOKENS) ** 0.5), 256.0, ((0, 128),), jnp.float32),
        "gains_second": jnp.clip(jnp.exp(math.log(30965.76) - 1.3768156 * jax.random.uniform(streams_of[17], (D, 2), jnp.float32) ** block_levels(streams_of[17], (D, 2), ((0, 128),), -0.2, 0.2)), 7815.168, 30965.76),
    }


@jax.custom_vjp
def low(v):
    return lax.optimization_barrier(v.astype(jnp.bfloat16)).astype(jnp.float32)

@jax.custom_vjp
def low_back(v):
    return v

def low_keep(v):
    return (low(v), None)

def low_pass(kept, grad):
    return (grad,)

def back_keep(v):
    return (v, None)

def back_low(kept, grad):
    return (low(grad),)
low.defvjp(low_keep, low_pass)
low_back.defvjp(back_keep, back_low)
norm_eps = 1e-05
rope_base = 10000.0
beta_one = 0.9
beta_two = 0.95
adam_eps = 1e-08
decay_rate = 0.1
rate_qkv = 0.05
rate_proj = 0.3
rate_gate_up = 0.04
rate_down = 0.04
rate_gains = 0.5

def rotary_tables(token_pos, half_dim):
    inv_freq = rope_base ** (-jnp.arange(half_dim, dtype=jnp.float32) * 2.0 / (2 * half_dim))
    angles = token_pos.astype(jnp.float32)[:, None] * inv_freq[None, :]
    return (jnp.cos(angles), jnp.sin(angles))

def rotate(field, cos_vals, sin_vals):
    half_dim = field.shape[-1] // 2
    first_half = field[..., :half_dim]
    second_half = field[..., half_dim:]
    cos_b = cos_vals[:, None, :]
    sin_b = sin_vals[:, None, :]
    return jnp.concatenate([first_half * cos_b - second_half * sin_b, second_half * cos_b + first_half * sin_b], axis=-1)

def matmul_high(lhs_mat, rhs_mat):
    return jnp.dot(lhs_mat, rhs_mat, precision=lax.Precision.HIGHEST, preferred_element_type=jnp.float32)

def norm_scale(field, gain_vals):
    return field * lax.rsqrt(lax.optimization_barrier(jnp.mean(field * field, axis=-1, keepdims=True)) + norm_eps) * gain_vals[None, :]

def attention(queries, key_rows, values, token_pos):
    length = queries.shape[0]
    group_size = HEADS // KV_HEADS
    scale_vals = HEAD_DIM ** (-0.5)
    query_heads = queries.reshape(length, KV_HEADS, group_size, HEAD_DIM).transpose(1, 2, 0, 3)
    key_heads = key_rows.transpose(1, 0, 2)
    value_heads = values.transpose(1, 0, 2)
    allowed = token_pos[None, :] <= token_pos[:, None]

    def one_head(head_args):
        q_head, k_head, v_head = head_args
        raw = jnp.einsum('gqd,kd->gqk', q_head, k_head, precision=lax.Precision.HIGHEST)
        scores = low_back(raw * scale_vals)
        scores = jnp.where(allowed[None, :, :], scores, -1e+30)
        row_top = lax.optimization_barrier(jnp.max(scores, axis=-1, keepdims=True))
        exp_vals = jnp.exp(scores - row_top)
        prob_vals = exp_vals / lax.optimization_barrier(jnp.sum(exp_vals, axis=-1, keepdims=True))
        return jnp.einsum('gqk,kd->gqd', low(prob_vals), v_head, precision=lax.Precision.HIGHEST)
    attended = lax.map(jax.checkpoint(one_head), (query_heads, key_heads, value_heads))
    return attended.transpose(2, 0, 1, 3).reshape(length, HEADS * HEAD_DIM)

def layer_forward(inputs, params, token_pos):
    qkv_w, proj_w, gate_up_w, down_w, gain_w = params
    qkv_low = low(qkv_w)
    proj_low = low(proj_w)
    gate_up_low = low(gate_up_w)
    down_low = low(down_w)
    gain_low = low(gain_w)
    length = inputs.shape[0]
    cos_vals, sin_vals = rotary_tables(token_pos, HEAD_DIM // 2)
    hidden_one = low(norm_scale(inputs, gain_low[:, 0]))
    projected = low_back(matmul_high(hidden_one, qkv_low))
    q_cols = HEADS * HEAD_DIM
    k_cols = KV_HEADS * HEAD_DIM
    queries = low(rotate(projected[:, :q_cols].reshape(length, HEADS, HEAD_DIM), cos_vals, sin_vals))
    key_rows = low(rotate(projected[:, q_cols:q_cols + k_cols].reshape(length, KV_HEADS, HEAD_DIM), cos_vals, sin_vals))
    values = low(projected[:, q_cols + k_cols:].reshape(length, KV_HEADS, HEAD_DIM))
    attended = attention(queries, key_rows, values, token_pos)
    merged = low(low_back(attended))
    middle = inputs + low_back(matmul_high(merged, proj_low))
    hidden_two = low(norm_scale(middle, gain_low[:, 1]))
    gate_up = low_back(matmul_high(hidden_two, gate_up_low))
    gate_vals = gate_up[:, :FF]
    up_vals = gate_up[:, FF:]
    product = low(jax.nn.silu(gate_vals) * up_vals)
    return middle + low_back(matmul_high(product, down_low))

def adam_step(weight, moment_one, moment_two, gradient, step_rate, weight_decay):
    first_new = beta_one * moment_one + (1.0 - beta_one) * gradient
    second_new = beta_two * moment_two + (1.0 - beta_two) * gradient * gradient
    first_hat = first_new / (1.0 - beta_one ** STEP)
    second_hat = second_new / (1.0 - beta_two ** STEP)
    weight_new = weight - step_rate * (first_hat / (jnp.sqrt(second_hat) + adam_eps) + weight_decay * weight)
    return (first_new, second_new, weight_new)

def reference(layer_input, out_cotangent, positions, qkv_weight, qkv_first, qkv_second, proj_weight, proj_first, proj_second, gate_up_weight, gate_up_first, gate_up_second, down_weight, down_first, down_second, norm_gains, gains_first, gains_second):
    params = (qkv_weight, proj_weight, gate_up_weight, down_weight, norm_gains)

    def one_sequence(grad_total, seq_item):
        seq_inputs, seq_cot, seq_pos = seq_item
        result, pullback = jax.vjp(lambda inputs, weights: layer_forward(inputs, weights, seq_pos), seq_inputs.astype(jnp.float32), params)
        grad_in, grad_params = pullback(seq_cot.astype(jnp.float32))
        grad_total = jax.tree.map(lambda acc_grad, new_grad: acc_grad + new_grad, grad_total, grad_params)
        return (grad_total, (result.astype(jnp.bfloat16), grad_in))
    zero_grads = jax.tree.map(jnp.zeros_like, params)
    grad_sum, (outputs, grad_inputs) = lax.scan(one_sequence, zero_grads, (layer_input, out_cotangent, positions))
    grad_qkv, grad_proj, grad_gate_up, grad_down, grad_gains = grad_sum
    qkv_new = adam_step(qkv_weight, qkv_first, qkv_second, grad_qkv, rate_qkv, decay_rate)
    proj_new = adam_step(proj_weight, proj_first, proj_second, grad_proj, rate_proj, decay_rate)
    gate_up_new = adam_step(gate_up_weight, gate_up_first, gate_up_second, grad_gate_up, rate_gate_up, decay_rate)
    down_new = adam_step(down_weight, down_first, down_second, grad_down, rate_down, decay_rate)
    gains_new = adam_step(norm_gains, gains_first, gains_second, grad_gains, rate_gains, 0.0)
    return (outputs, grad_inputs, qkv_new[0], qkv_new[1], qkv_new[2], proj_new[0], proj_new[1], proj_new[2], gate_up_new[0], gate_up_new[1], gate_up_new[2], down_new[0], down_new[1], down_new[2], gains_new[0], gains_new[1], gains_new[2])
```

```python
import jax
import jax.numpy as jnp
from jax import lax
from jax.sharding import Mesh
from jax.sharding import PartitionSpec as P

HEADS = 32
KV_HEADS = 4
HEAD_DIM = 64
GROUP = HEADS // KV_HEADS
STEP = 10

norm_eps = 1e-05
rope_base = 10000.0
beta_one = 0.9
beta_two = 0.95
adam_eps = 1e-08
decay_rate = 0.1
rate_qkv = 0.05
rate_proj = 0.3
rate_gate_up = 0.04
rate_down = 0.04
rate_gains = 0.5

SIZES = {"z": 4, "yh": 2, "x": 4, "yl": 2, "c": 2}
SEQ = ("z", "yh")
CTX = ("x", "yl", "c")
ROWS = SEQ + CTX
OWNERS = ("yh", "x", "yl", "c")
RING_Y = ("yh", "yl")
NZ = 4
NCTX = 16
BF = jnp.bfloat16
F32 = jnp.float32


def axis_size(axis):
    if isinstance(axis, str):
        return SIZES[axis]
    count = 1
    for name in axis:
        count *= SIZES[name]
    return count


def send(field, axis, step):
    count = axis_size(axis)
    return lax.ppermute(field, axis, [(i, (i + step) % count) for i in range(count)])


def gather_z(field):
    return [field] + [send(field, "z", step) for step in range(1, NZ)]


def return_z(parts):
    return [send(parts[step], "z", -step) for step in range(1, NZ)]


def dot(lhs, rhs):
    return jnp.dot(lhs, rhs, preferred_element_type=F32)


def dot_t(lhs, rhs):
    return lax.dot_general(lhs, rhs, (((1,), (1,)), ((), ())), preferred_element_type=F32)


def t_dot(lhs, rhs):
    return lax.dot_general(lhs, rhs, (((0,), (0,)), ((), ())), preferred_element_type=F32)


def rotary_tables(token_pos):
    half_dim = HEAD_DIM // 2
    inv_freq = rope_base ** (-jnp.arange(half_dim, dtype=F32) * 2.0 / (2 * half_dim))
    angles = token_pos.astype(F32)[:, None] * inv_freq[None, :]
    return (jnp.cos(angles), jnp.sin(angles))


def rotate(field, cos_vals, sin_vals):
    half_dim = field.shape[-1] // 2
    first_half = field[..., :half_dim]
    second_half = field[..., half_dim:]
    cos_b = cos_vals[:, None, :]
    sin_b = sin_vals[:, None, :]
    return jnp.concatenate(
        [first_half * cos_b - second_half * sin_b, second_half * cos_b + first_half * sin_b],
        axis=-1,
    )


def norm_scale(field):
    return lax.rsqrt(jnp.mean(field * field, axis=-1, keepdims=True) + norm_eps)


def norm_back(grad_normed, normed, scale_vals):
    row_inner = jnp.mean(grad_normed * normed, axis=-1, keepdims=True)
    return scale_vals * (grad_normed - normed * row_inner)


def attend_forward(q_rows, k_rows, v_rows, allowed):
    scores = dot_t(q_rows, k_rows) * HEAD_DIM ** (-0.5)
    scores = jnp.where(allowed, scores, -1e30)
    row_top = jnp.max(scores, axis=-1, keepdims=True)
    exp_vals = jnp.exp(scores - row_top)
    row_total = jnp.sum(exp_vals, axis=-1, keepdims=True)
    prob_vals = (exp_vals / row_total).astype(BF)
    return (dot(prob_vals, v_rows), row_top + jnp.log(row_total))


def attend_backward(q_rows, k_rows, v_rows, g_rows, log_sums, allowed):
    scale = HEAD_DIM ** (-0.5)
    scores = dot_t(q_rows, k_rows) * scale
    scores = jnp.where(allowed, scores, -1e30)
    prob_vals = jnp.exp(scores - log_sums)
    grad_probs = dot_t(g_rows, v_rows)
    row_inner = jnp.sum(prob_vals * grad_probs, axis=-1, keepdims=True)
    grad_scores = (prob_vals * (grad_probs - row_inner)).astype(BF)
    return (
        dot(grad_scores, k_rows) * scale,
        t_dot(grad_scores, q_rows) * scale,
        t_dot(prob_vals.astype(BF), g_rows),
    )


def adam_step(weight, moment_one, moment_two, gradient, step_rate, weight_decay):
    first_new = beta_one * moment_one + (1.0 - beta_one) * gradient
    second_new = beta_two * moment_two + (1.0 - beta_two) * gradient * gradient
    first_hat = first_new / (1.0 - beta_one**STEP)
    second_hat = second_new / (1.0 - beta_two**STEP)
    weight_new = weight - step_rate * (
        first_hat / (jnp.sqrt(second_hat) + adam_eps) + weight_decay * weight
    )
    return (first_new, second_new, weight_new)


def gather_rows(shard):
    return lax.all_gather(shard, OWNERS, axis=0, tiled=False)


def deal(field, axis, dim):
    count = axis_size(axis)
    me = lax.axis_index(axis)
    own = lax.dynamic_index_in_dim(field, me, dim, keepdims=False)
    total = own.astype(F32)
    for step in range(1, count):
        block = lax.dynamic_index_in_dim(field, lax.rem(me + step, count), dim, keepdims=False)
        total = total + send(block.astype(BF), axis, step).astype(F32)
    return total


def scatter_rows(field):
    pre, _, _, _, _, rows, cols = field.shape
    field = deal(field, "c", 4).astype(BF)
    half = cols // 2
    one = deal(field[..., :half], "x", 2).astype(BF)
    one = deal(one.reshape(pre, 4, rows, half), RING_Y, 1)
    two = field[..., half:].transpose(0, 1, 3, 2, 4, 5).reshape(pre, 4, 4, rows, half)
    two = deal(two, RING_Y, 1).astype(BF)
    two = deal(two, "x", 1)
    return jnp.concatenate([one, two], axis=-1)


def on_device(
    layer_input,
    out_cotangent,
    positions,
    qkv_weight,
    qkv_first,
    qkv_second,
    proj_weight,
    proj_first,
    proj_second,
    gate_up_weight,
    gate_up_first,
    gate_up_second,
    down_weight,
    down_first,
    down_second,
    norm_gains,
    gains_first,
    gains_second,
):
    toks = layer_input.shape[1]
    width = layer_input.shape[2]
    length = positions.shape[1]
    q_cols = GROUP * HEAD_DIM
    own_rows = qkv_weight.shape[0]
    hidden = gate_up_weight.shape[1] // (2 * NZ)
    ctx = lax.axis_index(CTX)

    gains_low = norm_gains.astype(BF).astype(F32)
    qkv_low = qkv_weight.astype(BF).astype(F32)
    gate_up_low = gate_up_weight.astype(BF).astype(F32)

    tokens = gather_z(layer_input[0])
    all_pos = jnp.stack(gather_z(positions[0]))

    qkv_scaled = (qkv_low * gains_low[:, :1]).astype(BF)
    q_part, k_part, v_part = jnp.split(
        qkv_scaled, [HEADS * HEAD_DIM, (HEADS + KV_HEADS) * HEAD_DIM], axis=1
    )
    qkv_parts = jnp.concatenate(
        [t.reshape(own_rows, NZ, -1).transpose(1, 0, 2) for t in (q_part, k_part, v_part)], axis=2
    )
    qkv_parts = lax.all_to_all(qkv_parts, "z", split_axis=0, concat_axis=0)
    qkv_use = gather_rows(qkv_parts).transpose(1, 0, 2, 3).reshape(width, -1)
    proj_use = gather_rows(proj_weight.astype(BF)).reshape(q_cols, width)
    gate_up_scaled = (gate_up_low * gains_low[:, 1:]).astype(BF)
    gate_up_parts = (
        gate_up_scaled.reshape(own_rows, 2, NZ, hidden).transpose(2, 0, 1, 3).reshape(NZ, own_rows, -1)
    )
    gate_up_parts = lax.all_to_all(gate_up_parts, "z", split_axis=0, concat_axis=0)
    gate_up_use = gather_rows(gate_up_parts).transpose(1, 0, 2, 3).reshape(width, -1)
    down_use = gather_rows(down_weight.astype(BF)).reshape(hidden, width)
    cotangents = jnp.concatenate(gather_z(out_cotangent[0]))

    own_pos = lax.dynamic_slice_in_dim(all_pos, ctx * toks, toks, axis=1)
    cos_vals, sin_vals = rotary_tables(own_pos.reshape(-1))
    inputs = jnp.concatenate(tokens).astype(F32)
    hidden_one = (inputs * norm_scale(inputs)).astype(BF)
    projected = dot(hidden_one, qkv_use)
    keys = rotate(projected[:, None, q_cols : q_cols + HEAD_DIM], cos_vals, sin_vals)[:, 0]
    key_values = jnp.concatenate([keys, projected[:, q_cols + HEAD_DIM :]], axis=1).astype(BF)
    key_values = lax.all_to_all(
        jnp.broadcast_to(key_values[None], (NCTX, NZ * toks, 2 * HEAD_DIM)),
        CTX,
        split_axis=0,
        concat_axis=0,
    )
    key_values = (
        key_values.reshape(NCTX, NZ, toks, 2 * HEAD_DIM)
        .transpose(1, 0, 2, 3)
        .reshape(NZ, length, 2 * HEAD_DIM)
    )
    queries = rotate(
        projected[:, :q_cols].reshape(NZ * toks, GROUP, HEAD_DIM), cos_vals, sin_vals
    ).astype(BF)
    queries = (
        queries.reshape(NZ, toks, GROUP, HEAD_DIM)
        .transpose(0, 2, 1, 3)
        .reshape(NZ, GROUP * toks, HEAD_DIM)
    )
    keys_all, values_all = key_values[..., :HEAD_DIM], key_values[..., HEAD_DIM:]

    attended, log_sums, masks, branch = [], [], [], []
    for part in (1, 2, 3, 0):
        allowed = all_pos[part][None, :] <= own_pos[part][:, None]
        allowed = jnp.broadcast_to(allowed[None], (GROUP, toks, length)).reshape(-1, length)
        out, log_sum = attend_forward(queries[part], keys_all[part], values_all[part], allowed)
        out = (
            out.reshape(GROUP, toks, HEAD_DIM).transpose(1, 0, 2).reshape(toks, q_cols).astype(BF)
        )
        masks.append(allowed)
        attended.append(out)
        log_sums.append(log_sum)
        branch.append(dot(out, proj_use))
    masks, attended, log_sums, branch = (
        [t[3], t[0], t[1], t[2]] for t in (masks, attended, log_sums, branch)
    )
    middle = layer_input[0].astype(F32) + branch[0]
    for got in return_z([t.astype(BF) for t in branch]):
        middle = middle + got.astype(F32)
    scale_two = norm_scale(middle)
    normed_two = middle * scale_two
    hidden_two = jnp.concatenate(gather_z(normed_two.astype(BF)))

    gate_up = dot(hidden_two, gate_up_use)
    gate_vals, up_vals = gate_up[:, :hidden], gate_up[:, hidden:]
    sig_vals = jax.nn.sigmoid(gate_vals)
    activated = gate_vals * sig_vals
    product = (activated * up_vals).astype(BF)
    grad_product = dot_t(cotangents, down_use)
    grad_gate = grad_product * up_vals * (sig_vals * (1.0 + gate_vals * (1.0 - sig_vals)))
    grad_up = grad_product * activated
    grad_gate_up = jnp.concatenate([grad_gate, grad_up], axis=1).astype(BF)
    grad_hidden = dot_t(grad_gate_up, gate_up_use).reshape(NZ, toks, width)
    grad_mid_norm = grad_hidden[0]
    for got in return_z([t.astype(BF) for t in grad_hidden]):
        grad_mid_norm = grad_mid_norm + got.astype(F32)
    terms = dot(product, down_use).reshape(NZ, toks, width)
    result = middle + terms[0]
    for got in return_z([t.astype(BF) for t in terms]):
        result = result + got.astype(F32)

    grad_down = t_dot(product, cotangents).astype(BF)
    grad_gate_up_w = t_dot(hidden_two, grad_gate_up).astype(BF)
    sum_down = scatter_rows(grad_down.reshape(1, 2, 4, 2, 2, -1, width))[0]
    sum_gate_up = scatter_rows(grad_gate_up_w.reshape(NZ, 2, 4, 2, 2, own_rows, 2 * hidden))
    sum_gate_up = lax.all_to_all(sum_gate_up.astype(BF), "z", split_axis=0, concat_axis=0)
    sum_gate_up = (
        sum_gate_up.astype(F32)
        .reshape(NZ, own_rows, 2, hidden)
        .transpose(1, 2, 0, 3)
        .reshape(own_rows, -1)
    )

    grad_result = out_cotangent[0].astype(F32)
    grad_middle = grad_result + norm_back(grad_mid_norm, normed_two, scale_two)
    grad_branch = gather_z(grad_middle.astype(BF))
    grad_q, grad_kv = [], []
    for part in range(NZ):
        grad_out = dot_t(grad_branch[part], proj_use).astype(BF)
        grad_out = (
            grad_out.reshape(toks, GROUP, HEAD_DIM).transpose(1, 0, 2).reshape(-1, HEAD_DIM)
        )
        one, two, three = attend_backward(
            queries[part],
            keys_all[part],
            values_all[part],
            grad_out,
            log_sums[part],
            masks[part],
        )
        grad_q.append(one.reshape(GROUP, toks, HEAD_DIM).transpose(1, 0, 2))
        grad_kv.append(jnp.concatenate([two, three], axis=1).astype(BF))
    grad_kv = (
        jnp.stack(grad_kv).reshape(NZ, NCTX, toks, 2 * HEAD_DIM).transpose(1, 0, 2, 3)
    )
    grad_kv = lax.all_to_all(grad_kv, CTX, split_axis=0, concat_axis=0)
    grad_kv = jnp.sum(grad_kv.astype(F32), axis=0).reshape(NZ * toks, 2 * HEAD_DIM)
    grad_q = rotate(jnp.concatenate(grad_q), cos_vals, -sin_vals).reshape(NZ * toks, q_cols)
    grad_k = rotate(grad_kv[:, None, :HEAD_DIM], cos_vals, -sin_vals)[:, 0]
    grad_projected = jnp.concatenate([grad_q, grad_k, grad_kv[:, HEAD_DIM:]], axis=1).astype(BF)
    grad_hidden_one = dot_t(grad_projected, qkv_use).reshape(NZ, toks, width)
    grad_in_norm = grad_hidden_one[0]
    for got in return_z([t.astype(BF) for t in grad_hidden_one]):
        grad_in_norm = grad_in_norm + got.astype(F32)
    own_inputs = layer_input[0].astype(F32)
    scale_one = norm_scale(own_inputs)
    input_grad = grad_middle + norm_back(grad_in_norm, own_inputs * scale_one, scale_one)

    grad_proj = t_dot(jnp.concatenate(attended), jnp.concatenate(grad_branch)).astype(BF)
    sum_proj = scatter_rows(grad_proj.reshape(1, 2, 4, 2, 2, own_rows, width))[0]
    grad_qkv = t_dot(hidden_one, grad_projected).astype(BF)
    sum_qkv = scatter_rows(grad_qkv.reshape(NZ, 2, 4, 2, 2, own_rows, -1))
    sum_qkv = lax.all_to_all(sum_qkv.astype(BF), "z", split_axis=0, concat_axis=0).astype(F32)
    sum_qkv = jnp.concatenate(
        [
            t.transpose(1, 0, 2).reshape(own_rows, -1)
            for t in jnp.split(sum_qkv, [q_cols, q_cols + HEAD_DIM], axis=2)
        ],
        axis=1,
    )

    sum_gains = jnp.stack(
        [jnp.sum(qkv_low * sum_qkv, axis=1), jnp.sum(gate_up_low * sum_gate_up, axis=1)], axis=1
    )
    sum_qkv = sum_qkv * gains_low[:, :1]
    sum_gate_up = sum_gate_up * gains_low[:, 1:]
    qkv_new = adam_step(qkv_weight, qkv_first, qkv_second, sum_qkv, rate_qkv, decay_rate)
    proj_new = adam_step(proj_weight, proj_first, proj_second, sum_proj, rate_proj, decay_rate)
    gate_up_new = adam_step(
        gate_up_weight, gate_up_first, gate_up_second, sum_gate_up, rate_gate_up, decay_rate
    )
    down_new = adam_step(down_weight, down_first, down_second, sum_down, rate_down, decay_rate)
    gains_new = adam_step(norm_gains, gains_first, gains_second, sum_gains, rate_gains, 0.0)
    return (
        result.astype(BF)[None],
        input_grad[None],
        *qkv_new,
        *proj_new,
        *gate_up_new,
        *down_new,
        *gains_new,
    )


def solution(mesh):
    inner = Mesh(mesh.devices.reshape(tuple(SIZES.values())), tuple(SIZES))
    rows = P(ROWS, None)
    acts = P(SEQ, CTX, None)
    return jax.shard_map(
        on_device,
        mesh=inner,
        in_specs=(acts, acts, P(SEQ, None)) + (rows,) * 15,
        out_specs=(acts, acts) + (rows,) * 15,
        check_vma=False,
    )
```
